256 devices in a mesh: hist: 4 (over y), tok: 8 (over x, core), cand: 8 (over z).
Axes of the slice: x: 4, y: 4, z: 8, core: 2. Of those that a mesh axis runs over, the one named last changes fastest.
Arguments:
- features: bfloat16 [1024, 16, 2048], P('cand', 'tok'), may hold values from -6 to 6
- query_weight: bfloat16 [16, 2048, 128], P('tok'), may hold values from -0.125 to 0.125
- output_weight: bfloat16 [16, 128, 2048], P('tok'), may hold values from -0.5 to 0.5
- history: bfloat16 [16, 10240, 128], P('cand', 'hist'), may hold values from -500 to 500
- actions: int32 [16, 10240], P('cand', 'hist'), may hold values from 0 to 15
- lengths: int32 [16], P('cand'), may hold values from 1 to 10240, as said below
- cand_user: int32 [1024], P('cand'), may hold values from 0 to 15, as said below
- key_weight: bfloat16 [128, 128], replicated, may hold values from -0.5 to 0.5
- action_table: bfloat16 [16, 128], replicated, may hold values from -3 to 3
- value_weight: bfloat16 [128, 128], replicated, may hold values from -0.5 to 0.5
- gate_weight: bfloat16 [16, 2048, 8192], P('tok', None, ('hist', 'cand')), may hold values from -0.125 to 0.125
- up_weight: bfloat16 [16, 2048, 8192], P('tok', None, ('hist', 'cand')), may hold values from -0.125 to 0.125
- down_weight: bfloat16 [16, 8192, 2048], P('tok', ('hist', 'cand')), may hold values from -0.25 to 0.25
- tower_weight: bfloat16 [16, 2048, 256], P('tok'), may hold values from -0.03125 to 0.03125
- tower_bias: float32 [256], replicated, may hold values from -4 to 4
- head_weight: bfloat16 [256, 4], replicated, may hold values from -0.375 to 0.375
Outputs:
- layer_out: bfloat16 [1024, 16, 2048], P(('hist', 'cand'), 'tok')
- task_scores: float32 [1024, 4], P(('hist', 'cand'))
The draws below stay inside these ranges and needn't reach their ends.
Inputs may be any that keep to these rules, and one draw needn't show every extreme that they name: `lengths`: every user has at least one valid event, and some user has exactly 10240. `cand_user`: candidate b belongs to one of the 2 users numbered from (b // 128) * 2 on.
All inputs are finite; a program needn't handle non-finite values.
Results may differ from the reference program's by a relative error of at most 0.015.
The reference program's roundings to bfloat16 on the way count: a program that leaves them out, or rounds other values in their place, can miss the bound.
Values may be sent and summed in bfloat16 or wider, within the bound.
No kernel may reach another device: no remote copies, remote signals or barrier semaphores. Data moves between devices by JAX's collectives and lax.ppermute only.
A program may use at most 128 MiB of HBM per device.

```python
import math
import jax
import jax.numpy as jnp
import numpy as np
from jax import lax

D = 2048
FEATS = 16
FF = 8192
DK = 128
DH = 128
ACTIONS = 16
TH = 256
TASKS = 4
CAND_DEV = 128
USR_DEV = 2
HEAD = 128
CANDS = 1024
USERS = 16
HIST_LEN = 10240


def draw_history(key, part):
    key = jax.random.fold_in(key, 7)
    jitter_key, drifts_key = jax.random.split(key, 2)
    jitter = jax.random.normal(jitter_key, (USERS, HIST_LEN, DH), jnp.float32)
    stretch = max(HIST_LEN // 10, 1)
    pieces = (HIST_LEN + stretch - 1) // stretch
    drifts = jax.random.normal(drifts_key, (USERS, pieces, DH), jnp.float32)
    piece_of = jnp.arange(HIST_LEN) // stretch
    events = jitter + jnp.take(drifts, piece_of, axis=1)
    return jnp.clip(events, -500.0, 500.0).astype(jnp.bfloat16)


def draw_lengths(key, part):
    key = jax.random.fold_in(key, 3)
    length_key, pick_key = jax.random.split(key)
    drawn = jax.random.randint(length_key, (USERS,), 1, HIST_LEN + 1, dtype=jnp.int32)
    chosen = jax.random.randint(pick_key, (), 0, USERS, dtype=jnp.int32)
    return jnp.where(jnp.arange(USERS, dtype=jnp.int32) == chosen, HIST_LEN, drawn).astype(jnp.int32)


def draw_cand_user(key, part):
    key = jax.random.fold_in(key, 5)
    local_pick = jax.random.randint(key, (CANDS,), 0, USR_DEV, dtype=jnp.int32)
    position = jnp.arange(CANDS, dtype=jnp.int32)
    assigned = position // CAND_DEV * USR_DEV + local_pick
    assigned = jnp.where(position == 0, 0, jnp.where(position == CANDS - 1, USERS - 1, assigned))
    return assigned.astype(jnp.int32)


def with_ends(entries, key, least, top_value):
    extent = entries.shape
    spot = [jax.random.randint(jax.random.fold_in(key, axis), (), 0, extent[axis]) for axis in range(len(extent))]
    entries = entries.at[tuple(spot)].set(least)
    longest = extent.index(max(extent))
    spot[longest] = (spot[longest] + 1) % extent[longest]
    return entries.at[tuple(spot)].set(top_value)


def strengthened(array, rng, source, target, shards_of, factor):
    owner, partner = [(jnp.arange(array.shape[axis_at]) // (array.shape[axis_at] // shards_of)).reshape([-1 if axis == axis_at else 1 for axis in range(array.ndim)]) for axis_at in (source, target)]
    chosen = jax.random.permutation(rng, shards_of)[partner]
    strong = (owner == chosen) | (owner == (partner + shards_of // 2) % shards_of)
    return jnp.where(strong, factor * array, array)


def steps_of(key, shape, cuts, smallest, high):
    def one(axis_at, shards_of):
        steps = jax.random.uniform(jax.random.fold_in(jax.random.fold_in(key, 6), axis_at), (shards_of,), jnp.float32, smallest / len(cuts), high / len(cuts))
        return jnp.repeat(jnp.exp(steps), shape[axis_at] // shards_of).reshape((-1,) + (1,) * (len(shape) - axis_at - 1))

    level = one(*cuts[0])
    for cut in cuts[1:]:
        level = level * one(*cut)
    return level


def rank_bounds(number_of, slope):
    loads = [(1 << 20) // math.isqrt(grade ** slope) + 1 for grade in range(1, number_of + 1)]
    scale = 1 + sum(loads) // (1 << 30)
    return np.cumsum(np.array([max(1, weight // scale) for weight in loads]))


def skewed_ids(rng, dims, number_of, slope):
    listing = rank_bounds(number_of, slope)
    pick = jax.random.randint(jax.random.fold_in(rng, 1), dims, 0, int(listing[number_of - 1]))
    standing = jnp.searchsorted(jnp.asarray(listing, jnp.int32), pick, side="right")
    return jax.random.permutation(jax.random.fold_in(rng, 2), number_of)[standing].astype(jnp.int32)


def normal_values(stream_key, extent, scale, bound, cuts=(), held_as=jnp.bfloat16):
    entries = scale * jax.random.normal(stream_key, extent, jnp.float32)
    if cuts:
        entries = entries * steps_of(stream_key, extent, cuts, -0.22, 0.18)
    return jnp.clip(entries, -bound, bound).astype(held_as)


def bell_draw_with(key, shape, deviation, reach, shards, heavy, kind=jnp.bfloat16):
    values = deviation * jax.random.normal(key, shape, jnp.float32)
    if shards:
        values = values * steps_of(key, shape, shards, -0.22, 0.18)
    return jnp.clip(strengthened(values, jax.random.fold_in(key, 3), *heavy), -reach, reach).astype(kind)


def setup_inputs(seed: int = 0) -> dict:
    key_list = jax.random.split(jax.random.key(seed), 17)
    return {
        "features": normal_values(key_list[0], (CANDS, FEATS, D), 1.0, 6.0, ((0, 8), (1, 8))),
        "query_weight": normal_values(key_list[1], (FEATS, D, DK), D ** -0.5, 0.125, ((0, 8),)),
        "output_weight": normal_values(key_list[2], (FEATS, DK, D), DK ** -0.5, 0.5, ((0, 8),)),
        "history": draw_history(jax.random.fold_in(key_list[16], 71), 0),
        "actions": with_ends(skewed_ids(key_list[4], (USERS, HIST_LEN), ACTIONS, 2), jax.random.fold_in(key_list[4], 3), 0, ACTIONS - 1).astype(jnp.int32),
        "lengths": draw_lengths(jax.random.fold_in(key_list[16], 71), 0),
        "cand_user": draw_cand_user(jax.random.fold_in(key_list[16], 71), 0),
        "key_weight": normal_values(key_list[7], (DH, DK), DH ** -0.5, 0.5),
        "action_table": normal_values(key_list[8], (ACTIONS, DK), 0.5, 3.0),
        "value_weight": normal_values(key_list[9], (DH, DK), DH ** -0.5, 0.5),
        "gate_weight": normal_values(key_list[10], (FEATS, D, FF), D ** -0.5, 0.125, ((0, 8), (2, 32))),
        "up_weight": normal_values(key_list[11], (FEATS, D, FF), D ** -0.5, 0.125, ((0, 8), (2, 32))),
        "down_weight": bell_draw_with(key_list[12], (FEATS, FF, D), (FF // 4) ** -0.5, 0.25, ((0, 8), (1, 32)), (1, 2, 32, 2.75)),
        "tower_weight": normal_values(key_list[13], (FEATS, D, TH), (FEATS * D) ** -0.5, 0.03125, ((0, 8),)),
        "tower_bias": normal_values(key_list[14], (TH,), 1.0, 4.0, (), jnp.float32),
        "head_weight": normal_values(key_list[15], (TH, TASKS), TH ** -0.5, 0.375),
    }


EPS = 1e-06

def reference(features, query_weight, output_weight, history, actions, lengths, cand_user, key_weight, action_table, value_weight, gate_weight, up_weight, down_weight, tower_weight, tower_bias, head_weight):
    widened_hist = history.astype(jnp.float32)
    event_keys = (jnp.einsum('ulh,hk->ulk', widened_hist, key_weight.astype(jnp.float32)) + jnp.take(action_table, actions, axis=0).astype(jnp.float32)).astype(jnp.bfloat16)
    normed_history = (widened_hist * lax.rsqrt(lax.optimization_barrier(jnp.mean(widened_hist * widened_hist, axis=-1, keepdims=True)) + EPS)).astype(jnp.bfloat16)
    event_values = jnp.einsum('ulh,hk->ulk', normed_history.astype(jnp.float32), value_weight.astype(jnp.float32)).astype(jnp.bfloat16)
    queries = jnp.einsum('btd,tdk->btk', features.astype(jnp.float32), query_weight.astype(jnp.float32)).astype(jnp.bfloat16)
    positions = jnp.arange(HIST_LEN, dtype=jnp.int32)

    def attend(entry_pair):
        one_query, user_index = entry_pair
        user_keys = lax.dynamic_index_in_dim(event_keys, user_index, 0, keepdims=False)
        user_values = lax.dynamic_index_in_dim(event_values, user_index, 0, keepdims=False).astype(jnp.float32)
        user_length = lax.dynamic_index_in_dim(lengths, user_index, 0, keepdims=False)
        live_mask = (positions < user_length)[None, :]
        scores = jnp.dot(one_query, user_keys.T, preferred_element_type=jnp.float32) * (1.5 * DK ** (-0.5))
        filled = jnp.where(live_mask, scores, -1e+30)
        row_max = lax.optimization_barrier(jnp.max(filled, axis=1, keepdims=True))
        weights = jnp.where(live_mask, jnp.exp(filled - row_max), 0.0)
        row_total = lax.optimization_barrier(jnp.sum(weights, axis=1, keepdims=True))
        weighted = jnp.dot(weights, user_values, precision=lax.Precision.HIGHEST)
        return (weighted / row_total).astype(jnp.bfloat16)
    attended = lax.map(attend, (queries, cand_user))
    token_input = (features.astype(jnp.float32) + jnp.einsum('btk,tkd->btd', attended.astype(jnp.float32), output_weight.astype(jnp.float32))).astype(jnp.bfloat16)
    mixed = jnp.transpose(token_input.reshape(CANDS, FEATS, FEATS, HEAD), (0, 2, 1, 3)).reshape(CANDS, FEATS, D)

    def feed(entry_four):
        token_rows, w_gate, w_up, w_down = entry_four
        widened = token_rows.astype(jnp.float32)
        normed = (widened * lax.rsqrt(lax.optimization_barrier(jnp.mean(widened * widened, axis=-1, keepdims=True)) + EPS)).astype(jnp.bfloat16)
        gate_values = jnp.dot(normed, w_gate, preferred_element_type=jnp.float32)
        up_values = jnp.dot(normed, w_up, preferred_element_type=jnp.float32)
        hidden = (jax.nn.silu(gate_values) * up_values).astype(jnp.bfloat16)
        return (widened + jnp.dot(hidden, w_down, preferred_element_type=jnp.float32)).astype(jnp.bfloat16)
    layer_out = jnp.swapaxes(lax.map(feed, (jnp.swapaxes(mixed, 0, 1), gate_weight, up_weight, down_weight)), 0, 1)
    tower_pre = jnp.einsum('bsd,sdh->bh', layer_out.astype(jnp.float32), tower_weight.astype(jnp.float32)) + tower_bias
    tower_hidden = jax.nn.silu(tower_pre).astype(jnp.bfloat16)
    task_scores = jnp.dot(tower_hidden, head_weight, preferred_element_type=jnp.float32)
    return (layer_out, task_scores)
```

```python
import jax
import jax.numpy as jnp
from jax import lax
from jax.experimental import pallas as pl
from jax.experimental.pallas import tpu as pltpu
from jax.sharding import PartitionSpec as P

EPS = 1e-06
DK = 128
ACTIONS = 16
HIST, TOK, CAND = 4, 8, 8
SCALE = 1.5 * DK ** (-0.5) * 1.4426950408889634
CHUNK = 512
F32 = jnp.float32
BF16 = jnp.bfloat16


def dot(a, b, dims=((1,), (0,))):
    return lax.dot_general(a, b, (dims, ((), ())), preferred_element_type=F32)


def attention_kernel(limit_ref, q_ref, owner_ref, hist_ref, act_ref, kwt_ref, tabt_ref, vw_ref, out_ref, m_ref, l_ref, acc_ref):
    step = pl.program_id(0)

    @pl.when(step == 0)
    def _():
        m_ref[...] = jnp.full_like(m_ref, -1e29)
        l_ref[...] = jnp.zeros_like(l_ref)
        acc_ref[...] = jnp.zeros_like(acc_ref)

    first = owner_ref[...] == 0
    q = q_ref[...]
    where = lax.broadcasted_iota(jnp.int32, (1, CHUNK), 1) + step * CHUNK
    scores, values = [], []
    for u in range(2):
        h = hist_ref[u]
        kinds = lax.broadcasted_iota(jnp.int32, (ACTIONS, CHUNK), 0)
        onehot = jnp.where(kinds == act_ref[u : u + 1, :], 1.0, 0.0).astype(BF16)
        keys = dot(kwt_ref[...], h, ((1,), (1,))) + dot(tabt_ref[...], onehot)
        s = dot(q, keys.astype(BF16)) * SCALE
        scores.append(jnp.where(where < limit_ref[u], s, -1e30))
        wide = h.astype(F32)
        normed = wide * lax.rsqrt(jnp.mean(wide * wide, axis=1, keepdims=True) + EPS)
        values.append(dot(normed.astype(BF16), vw_ref[...]).astype(BF16))
    s = jnp.where(first, scores[0], scores[1])
    m_old = m_ref[...]
    m_new = jnp.maximum(m_old, jnp.max(s, axis=1, keepdims=True))
    p = jnp.exp2(s - m_new)
    fade = jnp.exp2(m_old - m_new)
    m_ref[...] = m_new
    l_ref[...] = l_ref[...] * fade + jnp.sum(p, axis=1, keepdims=True)
    high = p.astype(BF16)
    low = (p - high.astype(F32)).astype(BF16)
    zero = jnp.zeros_like(high)
    total = acc_ref[...] * fade
    for part in (high, low):
        total += dot(jnp.where(first, part, zero), values[0])
        total += dot(jnp.where(first, zero, part), values[1])
    acc_ref[...] = total

    @pl.when(step == pl.num_programs(0) - 1)
    def _():
        out_ref[0:256, :] = acc_ref[...]
        for n, ref in ((256, m_ref), (258, l_ref)):
            row = jnp.transpose(jnp.broadcast_to(ref[...], (256, 128)))
            out_ref[n : n + 1, :] = row[0:1, 0:128]
            out_ref[n + 1 : n + 2, :] = row[0:1, 128:256]
        out_ref[260:264, :] = jnp.zeros((4, 128), F32)


def attention(limits, queries, owner, history, actions, kwt, tabt, vw):
    steps = history.shape[1] // CHUNK
    whole = lambda *shape: pl.BlockSpec(shape, lambda i, lim: (0,) * len(shape))
    return pl.pallas_call(
        attention_kernel,
        out_shape=jax.ShapeDtypeStruct((264, 128), F32),
        grid_spec=pltpu.PrefetchScalarGridSpec(
            num_scalar_prefetch=1,
            grid=(steps,),
            in_specs=[
                whole(256, 128),
                whole(256, 1),
                pl.BlockSpec((2, CHUNK, 128), lambda i, lim: (0, i, 0)),
                pl.BlockSpec((2, CHUNK), lambda i, lim: (0, i)),
                whole(128, 128),
                whole(128, ACTIONS),
                whole(128, 128),
            ],
            out_specs=whole(264, 128),
            scratch_shapes=[pltpu.VMEM((256, 1), F32), pltpu.VMEM((256, 1), F32), pltpu.VMEM((256, 128), F32)],
        ),
        compiler_params=pltpu.CompilerParams(dimension_semantics=("arbitrary",), vmem_limit_bytes=24 << 20),
        cost_estimate=pl.CostEstimate(flops=2_000_000_000, bytes_accessed=2_000_000, transcendentals=700_000),
        name="attention",
    )(limits, queries, owner, history, actions, kwt, tabt, vw)


def merge_kernel(p0, p1, p2, p3, feat_ref, ow_ref, out_ref):
    parts = (p0, p1, p2, p3)

    def column(ref, n):
        rows = [jnp.transpose(jnp.broadcast_to(ref[n + i : n + i + 1, :], (128, 128))) for i in range(2)]
        return jnp.concatenate(rows, axis=0)

    maxima = [column(ref, 256) for ref in parts]
    top = jnp.maximum(jnp.maximum(maxima[0], maxima[1]), jnp.maximum(maxima[2], maxima[3]))
    total, weighted = 0.0, 0.0
    for ref, m in zip(parts, maxima):
        fade = jnp.exp2(m - top)
        total += column(ref, 258) * fade
        weighted += ref[0:256, :] * fade
    attended = (weighted / total).astype(BF16)
    for j in range(2):
        update = dot(attended[j * 128 : (j + 1) * 128], ow_ref[j])
        tokens = (feat_ref[j].astype(F32) + update).astype(BF16)
        for x in range(4):
            for k in range(2):
                for m in range(4):
                    out_ref[2 * x + k, m * 16 : (m + 1) * 16, j * 128 : (j + 1) * 128] = tokens[
                        m * 32 + k * 16 : m * 32 + k * 16 + 16, x * 128 : (x + 1) * 128
                    ]


def merge(parts, feats, ow):
    return pl.pallas_call(
        merge_kernel,
        out_shape=jax.ShapeDtypeStruct((8, 64, 256), BF16),
        compiler_params=pltpu.CompilerParams(vmem_limit_bytes=16 << 20),
        cost_estimate=pl.CostEstimate(flops=70_000_000, bytes_accessed=1_500_000, transcendentals=150_000),
        name="merge",
    )(*parts, feats, ow)


def ffn_kernel(x_ref, *refs):
    packs, out_ref = refs[:8], refs[8]
    gu, dn, normed, hidden, gu_sem, dn_sem = refs[9:]
    gu_copies = [pltpu.make_async_copy(packs[p].at[pl.ds(0, 16)], gu.at[p], gu_sem.at[p]) for p in range(8)]
    dn_copies = [
        pltpu.make_async_copy(packs[p].at[pl.ds(16, 8)], dn.at[:, pl.ds(p * 128, 128), :], dn_sem.at[p])
        for p in range(8)
    ]
    for copy in gu_copies + dn_copies:
        copy.start()
    for zb in range(8):
        wide = jnp.concatenate([x_ref[zb, s] for s in range(8)], axis=1).astype(F32)
        rows = (wide * lax.rsqrt(jnp.mean(wide * wide, axis=1, keepdims=True) + EPS)).astype(BF16)
        for m in range(4):
            to = ((zb % 2) * 4 + m) * 4 + zb // 2
            normed[to * 16 : (to + 1) * 16, :] = rows[m * 16 : (m + 1) * 16]
    for p in range(8):
        gu_copies[p].wait()
        both = dot(normed[...], gu[p].reshape(2048, 256))
        gate, up = both[:, :128], both[:, 128:]
        hidden[:, p * 128 : (p + 1) * 128] = (gate / (1.0 + jnp.exp(-gate)) * up).astype(BF16)
    for copy in dn_copies:
        copy.wait()
    for g in range(8):
        out_ref[:, g * 256 : (g + 1) * 256] = dot(hidden[...], dn[g]).astype(BF16)


def feed_forward(x, packs):
    return pl.pallas_call(
        ffn_kernel,
        out_shape=jax.ShapeDtypeStruct((512, 2048), BF16),
        in_specs=[pl.BlockSpec(memory_space=pltpu.VMEM)] + [pl.BlockSpec(memory_space=pl.ANY)] * 8,
        out_specs=pl.BlockSpec(memory_space=pltpu.VMEM),
        scratch_shapes=[
            pltpu.VMEM((8, 16, 128, 256), BF16),
            pltpu.VMEM((8, 1024, 256), BF16),
            pltpu.VMEM((512, 2048), BF16),
            pltpu.VMEM((512, 1024), BF16),
            pltpu.SemaphoreType.DMA((8,)),
            pltpu.SemaphoreType.DMA((8,)),
        ],
        compiler_params=pltpu.CompilerParams(vmem_limit_bytes=40 << 20),
        cost_estimate=pl.CostEstimate(flops=6_500_000_000, bytes_accessed=17_000_000, transcendentals=600_000),
        name="feed_forward",
    )(x, *packs)


def exchange_pairs(r, reverse):
    pairs = []
    for y in range(HIST):
        for t in range(TOK):
            x, c = t // 2, t % 2
            q = y ^ r
            source, target = (y, 2 * x + c), (2 * c + q // 2, 2 * x + q % 2)
            if reverse:
                source, target = target, source
            pairs.append((source[0] * TOK + source[1], target[0] * TOK + target[1]))
    return pairs


def shards(
    features,
    query_weight,
    output_weight,
    history,
    actions,
    lengths,
    cand_user,
    key_weight,
    action_table,
    value_weight,
    gate_weight,
    up_weight,
    down_weight,
    tower_weight,
    tower_bias,
    head_weight,
):
    y, tok, z = lax.axis_index("hist"), lax.axis_index("tok"), lax.axis_index("cand")
    core = tok % 2
    both = ("hist", "tok")

    packs = []
    for r in range(4):
        q = y ^ r
        j, k = q // 2, q % 2
        gate = lax.dynamic_slice(gate_weight, (j, 0, k * 128), (1, 2048, 128))
        up = lax.dynamic_slice(up_weight, (j, 0, k * 128), (1, 2048, 128))
        down = lax.dynamic_slice(down_weight, (j, k * 128, 0), (1, 128, 2048))
        pack = jnp.concatenate(
            [
                jnp.concatenate([gate, up], axis=2).reshape(16, 128, 256),
                jnp.swapaxes(down.reshape(128, 8, 256), 0, 1),
            ],
            axis=0,
        )
        packs.append(lax.ppermute(pack, both, exchange_pairs(r, False)))

    feats = jnp.swapaxes(features, 0, 1)
    queries = jnp.einsum("tbd,tdk->tbk", feats, query_weight, preferred_element_type=F32).astype(BF16)
    owner = cand_user - z * 2
    owner = jnp.concatenate([owner, owner])[:, None]
    part = attention(
        lengths - y * history.shape[1],
        queries.reshape(256, 128),
        owner,
        history,
        actions,
        key_weight.T,
        action_table.T,
        value_weight,
    )
    parts = [part] + [lax.ppermute(part, "hist", [(i, (i + d) % HIST) for i in range(HIST)]) for d in (1, 2, 3)]
    feat_sel = lax.dynamic_slice(feats.reshape(2, 128, 4, 4, 128), (0, 0, 0, y, 0), (2, 128, 4, 1, 128))
    ow_sel = lax.dynamic_slice(output_weight.reshape(2, 128, 4, 4, 128), (0, 0, 0, y, 0), (2, 128, 4, 1, 128))
    outgoing = merge(parts, feat_sel.reshape(2, 128, 512), ow_sel.reshape(2, 128, 512))
    mixed = lax.all_to_all(outgoing, "tok", split_axis=0, concat_axis=0, tiled=True)
    gathered = lax.all_gather(mixed[None], "cand", axis=0, tiled=True)

    swapped = [lax.ppermute(p, "tok", [(i, i ^ 1) for i in range(TOK)]) for p in packs]
    partial = feed_forward(gathered, packs + swapped)
    summed = lax.psum_scatter(partial, "cand", scatter_dimension=0, tiled=True)
    residual = lax.dynamic_slice(
        gathered.reshape(4, 2, 8, 4, 16, 256), (0, z // 4, 0, z % 4, 0, 0), (4, 1, 8, 1, 16, 256)
    ).reshape(4, 8, 16, 256)
    residual = jnp.swapaxes(residual, 1, 2).reshape(4, 16, 2048)
    block = (residual.astype(F32) + summed.reshape(4, 16, 2048).astype(F32)).astype(BF16)

    arrived = []
    mine = (y % 2) * 2 + core
    for r in range(4):
        send = lax.dynamic_index_in_dim(block, mine ^ r, 0, keepdims=False)
        arrived.append(lax.ppermute(send, both, exchange_pairs(r, True)))
    arrived = jnp.stack(arrived)
    quarters = [lax.dynamic_index_in_dim(arrived, y ^ q, 0, keepdims=False) for q in range(4)]
    tokens = [jnp.concatenate(quarters[2 * j : 2 * j + 2], axis=0) for j in range(2)]
    layer_out = jnp.stack(tokens, axis=1)

    tower_part = dot(tokens[0], tower_weight[0]) + dot(tokens[1], tower_weight[1])
    tower_sum = tower_part
    for d in range(1, TOK):
        tower_sum += lax.ppermute(tower_part, "tok", [(i, i ^ d) for i in range(TOK)])
    tower_hidden = jax.nn.silu(tower_sum + tower_bias).astype(BF16)
    task_scores = jnp.dot(tower_hidden, head_weight, preferred_element_type=F32)
    return (layer_out, task_scores)


def solution(mesh):
    in_specs = (
        P("cand", "tok", None),
        P("tok", None, None),
        P("tok", None, None),
        P("cand", "hist", None),
        P("cand", "hist"),
        P("cand"),
        P("cand"),
        P(),
        P(),
        P(),
        P("tok", None, ("hist", "cand")),
        P("tok", None, ("hist", "cand")),
        P("tok", ("hist", "cand"), None),
        P("tok", None, None),
        P(),
        P(),
    )
    out_specs = (P(("hist", "cand"), "tok", None), P(("hist", "cand"), None))
    return jax.shard_map(shards, mesh=mesh, in_specs=in_specs, out_specs=out_specs, check_vma=False)
```

```python
import jax
import jax.numpy as jnp
from jax import lax
from jax.experimental import pallas as pl
from jax.experimental.pallas import tpu as pltpu
from jax.sharding import PartitionSpec as P

EPS = 1e-06
DK = 128
ACTIONS = 16
HIST, TOK, CAND = 4, 8, 8
SCALE = 1.5 * DK ** (-0.5) * 1.4426950408889634
CHUNK = 512
F32 = jnp.float32
BF16 = jnp.bfloat16


def dot(a, b, dims=((1,), (0,))):
    return lax.dot_general(a, b, (dims, ((), ())), preferred_element_type=F32)


def pack_copies(gate_ref, up_ref, down_ref, held, sem):
    y = lax.axis_index("hist")
    copies = []
    for r in range(4):
        j, k = lax.rem(y // 2 + r // 2, 2), lax.rem(y + r, 2)
        half = pl.ds(pl.multiple_of(k * 128, 128), 128)
        moves = [
            (gate_ref.at[j, :, half], held.at[r, pl.ds(0, 2048), pl.ds(0, 128)]),
            (up_ref.at[j, :, half], held.at[r, pl.ds(0, 2048), pl.ds(128, 128)]),
        ]
        for g in range(8):
            moves.append((down_ref.at[j, half, pl.ds(g * 256, 256)], held.at[r, pl.ds(2048 + g * 128, 128), :]))
        copies += [pltpu.make_async_copy(source, target, sem.at[r, n]) for n, (source, target) in enumerate(moves)]
    return copies


def unload_copies(held, packs, sem):
    return [pltpu.make_async_copy(held.at[r], packs[r], sem.at[r, 10]) for r in range(4)]


def attention_kernel(length_ref, q_ref, user_ref, hist_ref, act_ref, kw_ref, tab_ref, vw_ref, gate_ref, up_ref, down_ref, *refs):
    out_ref, packs, (m_ref, l_ref, acc_ref, kwt_ref, tabt_ref, owner_ref, held, sem) = refs[0], refs[1:5], refs[5:]
    step = pl.program_id(0)
    events = CHUNK * pl.num_programs(0)
    offset = lax.axis_index("hist") * events + step * CHUNK

    @pl.when(step == 0)
    def _():
        for copy in pack_copies(gate_ref, up_ref, down_ref, held, sem):
            copy.start()
        m_ref[...] = jnp.full_like(m_ref, -1e29)
        l_ref[...] = jnp.zeros_like(l_ref)
        acc_ref[...] = jnp.zeros_like(acc_ref)
        kwt_ref[...] = jnp.transpose(kw_ref[...].astype(F32)).astype(BF16)
        tabt_ref[...] = jnp.transpose(tab_ref[...].astype(F32)).astype(BF16)
        user = jnp.transpose(jnp.broadcast_to(user_ref[...], (128, 128))) - lax.axis_index("cand") * 2
        owner_ref[0:128, :] = user[:, 0:1]
        owner_ref[128:256, :] = user[:, 0:1]

    @pl.when(step == 3)
    def _():
        for copy in pack_copies(gate_ref, up_ref, down_ref, held, sem):
            copy.wait()
        for copy in unload_copies(held, packs, sem):
            copy.start()

    first = owner_ref[...] == 0
    q = q_ref[...]
    where = lax.broadcasted_iota(jnp.int32, (1, CHUNK), 1) + offset
    scores, values = [], []
    for u in range(2):
        h = hist_ref[u]
        kinds = lax.broadcasted_iota(jnp.int32, (ACTIONS, CHUNK), 0)
        onehot = jnp.where(kinds == act_ref[u : u + 1, :], 1.0, 0.0).astype(BF16)
        keys = dot(kwt_ref[...], h, ((1,), (1,))) + dot(tabt_ref[...], onehot)
        s = dot(q, keys.astype(BF16)) * SCALE
        scores.append(jnp.where(where < length_ref[u], s, -1e30))
        wide = h.astype(F32)
        normed = wide * lax.rsqrt(jnp.mean(wide * wide, axis=1, keepdims=True) + EPS)
        values.append(dot(normed.astype(BF16), vw_ref[...]).astype(BF16))
    s = jnp.where(first, scores[0], scores[1])
    m_old = m_ref[...]
    m_new = jnp.maximum(m_old, jnp.max(s, axis=1, keepdims=True))
    p = jnp.exp2(s - m_new)
    fade = jnp.exp2(m_old - m_new)
    m_ref[...] = m_new
    l_ref[...] = l_ref[...] * fade + jnp.sum(p, axis=1, keepdims=True)
    acc_ref[...] = acc_ref[...] * fade + dot(p.astype(BF16), jnp.concatenate(values, axis=1))

    @pl.when(step == pl.num_programs(0) - 1)
    def _():
        weighted = jnp.where(first, acc_ref[:, 0:128], acc_ref[:, 128:256])
        out_ref[0:256, :] = (weighted / jnp.maximum(l_ref[...], 1e-30)).astype(BF16)
        for n, ref in ((256, m_ref), (272, l_ref)):
            row = jnp.transpose(jnp.broadcast_to(ref[...], (256, 128)))[0:1, :]
            rows = []
            for _ in range(3):
                piece = row.astype(BF16).astype(F32)
                row = row - piece
                rows += [piece[:, 0:128], piece[:, 128:256]]
            rows += [jnp.zeros((10, 128), F32)]
            out_ref[n : n + 16, :] = jnp.concatenate(rows, axis=0).astype(BF16)
        for copy in unload_copies(held, packs, sem):
            copy.wait()


def attention(lengths, queries, user, history, actions, kw, tab, vw, gate, up, down):
    steps = history.shape[1] // CHUNK
    whole = lambda *shape: pl.BlockSpec(shape, lambda i, lim: (0,) * len(shape))
    anywhere = pl.BlockSpec(memory_space=pl.ANY)
    return pl.pallas_call(
        attention_kernel,
        out_shape=[jax.ShapeDtypeStruct((288, 128), BF16)] + [jax.ShapeDtypeStruct((3072, 256), BF16)] * 4,
        grid_spec=pltpu.PrefetchScalarGridSpec(
            num_scalar_prefetch=1,
            grid=(steps,),
            in_specs=[
                whole(256, 128),
                whole(1, 128),
                pl.BlockSpec((2, CHUNK, 128), lambda i, lim: (0, i, 0)),
                pl.BlockSpec((2, CHUNK), lambda i, lim: (0, i)),
                whole(128, 128),
                whole(ACTIONS, 128),
                whole(128, 128),
                anywhere,
                anywhere,
                anywhere,
            ],
            out_specs=[whole(288, 128)] + [anywhere] * 4,
            scratch_shapes=[
                pltpu.VMEM((256, 1), F32),
                pltpu.VMEM((256, 1), F32),
                pltpu.VMEM((256, 256), F32),
                pltpu.VMEM((128, 128), BF16),
                pltpu.VMEM((128, ACTIONS), BF16),
                pltpu.VMEM((256, 1), jnp.int32),
                pltpu.VMEM((4, 3072, 256), BF16),
                pltpu.SemaphoreType.DMA((4, 11)),
            ],
        ),
        compiler_params=pltpu.CompilerParams(dimension_semantics=("arbitrary",), vmem_limit_bytes=58 << 20),
        cost_estimate=pl.CostEstimate(flops=1_000_000, bytes_accessed=100_000, transcendentals=1_000),
        name="attention",
    )(lengths, queries, user, history, actions, kw, tab, vw, gate, up, down)


def merge_kernel(p0, p1, p2, p3, feat_ref, ow_ref, out_ref):
    parts = (p0, p1, p2, p3)

    def column(ref, n):
        pieces = ref[n : n + 16, :].astype(F32)
        rows = pieces[0:2] + (pieces[2:4] + pieces[4:6])
        rows = [jnp.transpose(jnp.broadcast_to(rows[i : i + 1], (128, 128))) for i in range(2)]
        return jnp.concatenate(rows, axis=0)

    maxima = [column(ref, 256) for ref in parts]
    top = jnp.maximum(jnp.maximum(maxima[0], maxima[1]), jnp.maximum(maxima[2], maxima[3]))
    total, weighted = 0.0, 0.0
    for ref, m in zip(parts, maxima):
        share = column(ref, 272) * jnp.exp2(m - top)
        total += share
        weighted += ref[0:256, :].astype(F32) * share
    attended = (weighted / total).astype(BF16)
    y = lax.axis_index("hist")
    for x in range(4):
        columns = pl.ds(pl.multiple_of((4 * x + y) * 128, 128), 128)
        for j in range(2):
            update = dot(attended[j * 128 : (j + 1) * 128], ow_ref[j, :, columns])
            tokens = (feat_ref[j, :, columns].astype(F32) + update).astype(BF16)
            for k in range(2):
                for m in range(4):
                    out_ref[2 * x + k, m * 16 : (m + 1) * 16, j * 128 : (j + 1) * 128] = tokens[
                        m * 32 + k * 16 : m * 32 + k * 16 + 16
                    ]


def merge(parts, feats, ow):
    return pl.pallas_call(
        merge_kernel,
        out_shape=jax.ShapeDtypeStruct((8, 64, 256), BF16),
        compiler_params=pltpu.CompilerParams(vmem_limit_bytes=16 << 20),
        cost_estimate=pl.CostEstimate(flops=70_000_000, bytes_accessed=1_500_000, transcendentals=150_000),
        name="merge",
    )(*parts, feats, ow)


def hidden_part(normed, weights, hidden, p):
    both = dot(normed[...], weights)
    gate, up = both[:, :128], both[:, 128:]
    hidden[:, p * 128 : (p + 1) * 128] = (gate / (1.0 + jnp.exp(-gate)) * up).astype(BF16)


def first_kernel(x_ref, *refs):
    packs, (normed, hidden, gu, sem) = refs[:4], refs[4:]
    copies = [pltpu.make_async_copy(packs[p].at[pl.ds(0, 2048)], gu.at[p], sem.at[p]) for p in range(4)]
    for copy in copies:
        copy.start()
    z = lax.axis_index("cand")
    for zb in range(8):
        wide = jnp.concatenate([x_ref[zb, s] for s in range(8)], axis=1).astype(F32)
        rows = (wide * lax.rsqrt(jnp.mean(wide * wide, axis=1, keepdims=True) + EPS)).astype(BF16)
        for m in range(4):
            away = lax.rem((zb % 2) * 4 + m + 8 - z, 8)
            to = pl.multiple_of(away * 64 + (zb // 2) * 16, 16)
            normed[pl.ds(to, 16), :] = rows[m * 16 : (m + 1) * 16]
    for p in range(4):
        copies[p].wait()
        hidden_part(normed, gu[p], hidden, p)


def middle_kernel(normed, hidden_in, *refs):
    early, late, (so_far,), (hidden, gu, dn, gu_sem, dn_sem) = refs[:4], refs[4:6], refs[6:7], refs[7:]
    gu_copies = [pltpu.make_async_copy(late[p].at[pl.ds(0, 2048)], gu.at[p], gu_sem.at[p]) for p in range(2)]
    dn_copies = [
        pltpu.make_async_copy(pack.at[pl.ds(2048, 1024)], dn.at[p], dn_sem.at[p])
        for p, pack in enumerate(early + late)
    ]
    for copy in gu_copies + dn_copies:
        copy.start()
    for p in range(4):
        hidden[:, p * 128 : (p + 1) * 128] = hidden_in[:, p * 128 : (p + 1) * 128]
    for p in range(2):
        gu_copies[p].wait()
        hidden_part(normed, gu[p], hidden, 4 + p)
    for copy in dn_copies:
        copy.wait()
    for g in range(8):
        weights = jnp.concatenate([dn[p, g * 128 : (g + 1) * 128, :] for p in range(6)], axis=0)
        so_far[:, g * 256 : (g + 1) * 256] = dot(hidden[...], weights)


FAR = slice(256, 320)


def last_columns(normed, so_far, packs, hidden, g):
    weights = jnp.concatenate([pack[2048 + g * 128 : 2176 + g * 128, :] for pack in packs], axis=0)
    return (so_far[:, g * 256 : (g + 1) * 256] + dot(hidden[...], weights)).astype(BF16)


def far_kernel(normed, so_far, *refs):
    packs, (far_a, far_b, hidden) = refs[:2], refs[2:]
    for p in range(2):
        hidden_part(normed.at[FAR], packs[p][0:2048, :], hidden, p)
    for g in range(8):
        (far_a, far_b)[g // 4][:, (g % 4) * 256 : (g % 4 + 1) * 256] = last_columns(
            normed, so_far.at[FAR], packs, hidden, g
        )


def near_kernel(normed, so_far, *refs):
    packs, (near, hidden) = refs[:2], refs[2:]
    for p in range(2):
        hidden_part(normed, packs[p][0:2048, :], hidden, p)
    for g in range(8):
        columns = last_columns(normed, so_far, packs, hidden, g)
        for away in range(8):
            near[away, :, g * 256 : (g + 1) * 256] = columns[away * 64 : (away + 1) * 64]


def gate_kernel(*refs):
    pass


def gated(packs):
    shape = jax.ShapeDtypeStruct((3072, 256), BF16)
    n = len(packs)
    return pl.pallas_call(
        gate_kernel,
        out_shape=[shape] * n,
        in_specs=[pl.BlockSpec(memory_space=pl.ANY)] * n,
        out_specs=[pl.BlockSpec(memory_space=pl.ANY)] * n,
        input_output_aliases={i: i for i in range(n)},
        cost_estimate=pl.CostEstimate(flops=200_000_000_000, bytes_accessed=1000, transcendentals=0),
        name="gate",
    )(*packs)


VMEM_SPEC = pl.BlockSpec(memory_space=pltpu.VMEM)
ANY_SPEC = pl.BlockSpec(memory_space=pl.ANY)
FFN_PARAMS = pltpu.CompilerParams(vmem_limit_bytes=28 << 20)
FFN_COST = pl.CostEstimate(flops=3_000_000_000, bytes_accessed=8_000_000, transcendentals=300_000)


def feed_forward_first(x, packs):
    return pl.pallas_call(
        first_kernel,
        out_shape=[jax.ShapeDtypeStruct((512, 2048), BF16), jax.ShapeDtypeStruct((512, 512), BF16)],
        in_specs=[VMEM_SPEC] + [ANY_SPEC] * 4,
        out_specs=[VMEM_SPEC] * 2,
        scratch_shapes=[pltpu.VMEM((4, 2048, 256), BF16), pltpu.SemaphoreType.DMA((4,))],
        compiler_params=FFN_PARAMS,
        cost_estimate=FFN_COST,
        name="feed_forward_first",
    )(x, *packs)


def feed_forward_middle(normed, hidden, early, late):
    return pl.pallas_call(
        middle_kernel,
        out_shape=jax.ShapeDtypeStruct((512, 2048), F32),
        in_specs=[VMEM_SPEC] * 2 + [ANY_SPEC] * 6,
        out_specs=VMEM_SPEC,
        scratch_shapes=[
            pltpu.VMEM((512, 768), BF16),
            pltpu.VMEM((2, 2048, 256), BF16),
            pltpu.VMEM((6, 1024, 256), BF16),
            pltpu.SemaphoreType.DMA((2,)),
            pltpu.SemaphoreType.DMA((6,)),
        ],
        compiler_params=FFN_PARAMS,
        cost_estimate=FFN_COST,
        name="feed_forward_middle",
    )(normed, hidden, *early, *late)


def feed_forward_last(kernel, rows, outs, normed, so_far, packs, name):
    return pl.pallas_call(
        kernel,
        out_shape=[jax.ShapeDtypeStruct(shape, BF16) for shape in outs],
        in_specs=[VMEM_SPEC] * 4,
        out_specs=[VMEM_SPEC] * len(outs),
        scratch_shapes=[pltpu.VMEM((rows, 256), BF16)],
        compiler_params=FFN_PARAMS,
        cost_estimate=FFN_COST,
        name=name,
    )(normed, so_far, *packs)


def exchange_pairs(r, reverse):
    pairs = []
    for y in range(HIST):
        for t in range(TOK):
            x, c = t // 2, t % 2
            q = y ^ r
            source, target = (y, 2 * x + c), (2 * c + q // 2, 2 * x + q % 2)
            if reverse:
                source, target = target, source
            pairs.append((source[0] * TOK + source[1], target[0] * TOK + target[1]))
    return pairs


def shards(
    features,
    query_weight,
    output_weight,
    history,
    actions,
    lengths,
    cand_user,
    key_weight,
    action_table,
    value_weight,
    gate_weight,
    up_weight,
    down_weight,
    tower_weight,
    tower_bias,
    head_weight,
):
    y, tok, z = lax.axis_index("hist"), lax.axis_index("tok"), lax.axis_index("cand")
    core = tok % 2
    both = ("hist", "tok")

    feats = jnp.swapaxes(features, 0, 1)
    queries = jnp.einsum("tbd,tdk->tbk", feats, query_weight, preferred_element_type=F32).astype(BF16)
    part, *packs = attention(
        lengths,
        queries.reshape(256, 128),
        cand_user[None, :],
        history,
        actions,
        key_weight,
        action_table,
        value_weight,
        gate_weight,
        up_weight,
        down_weight,
    )
    parts = [part] + [lax.ppermute(part, "hist", [(i, (i + d) % HIST) for i in range(HIST)]) for d in (1, 2, 3)]
    packs, parts = lax.optimization_barrier((packs, parts))
    packs = [lax.ppermute(pack, both, exchange_pairs(r, False)) for r, pack in enumerate(packs)]

    outgoing = merge(parts, feats, output_weight)
    mixed = lax.all_to_all(outgoing, "tok", split_axis=0, concat_axis=0, tiled=True)
    gathered = lax.all_gather(mixed[None], "cand", axis=0, tiled=True)

    swap = lambda v: lax.ppermute(v, "tok", [(i, i ^ 1) for i in range(TOK)])
    early = list(gated(packs[:2]))
    late, early = lax.optimization_barrier((packs[2:], early))
    late = list(gated(late))
    own, swapped = early + late, [swap(v) for v in early + late]
    normed, hidden = feed_forward_first(gathered, own)
    so_far = feed_forward_middle(normed, hidden, own, swapped[:2])
    far_a, far_b = feed_forward_last(
        far_kernel, 64, ((64, 1024), (64, 1024)), normed, so_far, swapped[2:], "feed_forward_far"
    )
    (near,) = feed_forward_last(near_kernel, 512, ((8, 64, 2048),), normed, so_far, swapped[2:], "feed_forward_near")
    right = [(i, (i + 1) % CAND) for i in range(CAND)]
    left = [(i, (i - 1) % CAND) for i in range(CAND)]
    wide = lambda v: v.astype(F32)
    add = lambda v, w: (wide(v) + wide(w)).astype(BF16)
    up, down = lax.ppermute(far_a, "cand", right), lax.ppermute(far_b, "cand", left)
    up, down = jnp.pad(up, ((0, 0), (0, 1024))), jnp.pad(down, ((0, 0), (1024, 0)))
    for i in (3, 2, 1):
        up, down = lax.optimization_barrier((add(near[i], up), add(near[8 - i], down)))
        up, down = lax.ppermute(up, "cand", right), lax.ppermute(down, "cand", left)
    residual = lax.dynamic_slice(
        gathered.reshape(4, 2, 8, 4, 16, 256), (0, z // 4, 0, z % 4, 0, 0), (4, 1, 8, 1, 16, 256)
    ).reshape(4, 8, 16, 256)
    residual = jnp.swapaxes(residual, 1, 2).reshape(64, 2048)
    block = (wide(residual) + (wide(near[0]) + wide(up) + wide(down))).astype(BF16).reshape(4, 16, 2048)

    arrived = []
    mine = (y % 2) * 2 + core
    for r in range(4):
        send = lax.dynamic_index_in_dim(block, mine ^ r, 0, keepdims=False)
        arrived.append(lax.ppermute(send, both, exchange_pairs(r, True)))
    arrived = jnp.stack(arrived)
    quarters = [lax.dynamic_index_in_dim(arrived, y ^ q, 0, keepdims=False) for q in range(4)]
    tokens = [jnp.concatenate(quarters[2 * j : 2 * j + 2], axis=0) for j in range(2)]
    layer_out = jnp.stack(tokens, axis=1)

    tower_part = dot(tokens[0], tower_weight[0]) + dot(tokens[1], tower_weight[1])
    tower_part += swap(tower_part)
    tower_sum = tower_part
    for d in (2, 4, 6):
        tower_sum += lax.ppermute(tower_part, "tok", [(i, i ^ d) for i in range(TOK)])
    tower_hidden = jax.nn.silu(tower_sum + tower_bias).astype(BF16)
    task_scores = jnp.dot(tower_hidden, head_weight, preferred_element_type=F32)
    return (layer_out, task_scores)


def solution(mesh):
    in_specs = (
        P("cand", "tok", None),
        P("tok", None, None),
        P("tok", None, None),
        P("cand", "hist", None),
        P("cand", "hist"),
        P("cand"),
        P("cand"),
        P(),
        P(),
        P(),
        P("tok", None, ("hist", "cand")),
        P("tok", None, ("hist", "cand")),
        P("tok", ("hist", "cand"), None),
        P("tok", None, None),
        P(),
        P(),
    )
    out_specs = (P(("hist", "cand"), "tok", None), P(("hist", "cand"), None))
    return jax.shard_map(shards, mesh=mesh, in_specs=in_specs, out_specs=out_specs, check_vma=False)
```

```python
import jax
import jax.numpy as jnp
from jax import lax
from jax.experimental import pallas as pl
from jax.experimental.pallas import tpu as pltpu
from jax.sharding import PartitionSpec as P

EPS = 1e-06
DK = 128
ACTIONS = 16
HIST, TOK, CAND = 4, 8, 8
SCALE = 1.5 * DK ** (-0.5) * 1.4426950408889634
CHUNK = 512
F32 = jnp.float32
BF16 = jnp.bfloat16


def dot(a, b, dims=((1,), (0,))):
    return lax.dot_general(a, b, (dims, ((), ())), preferred_element_type=F32)


def pack_copies(gate_ref, up_ref, down_ref, held, sem):
    y = lax.axis_index("hist")
    copies = []
    for r in range(4):
        j, k = lax.rem(y // 2 + r // 2, 2), lax.rem(y + r, 2)
        half = pl.ds(pl.multiple_of(k * 128, 128), 128)
        moves = [
            (gate_ref.at[j, :, half], held.at[r, pl.ds(0, 2048), pl.ds(0, 128)]),
            (up_ref.at[j, :, half], held.at[r, pl.ds(0, 2048), pl.ds(128, 128)]),
        ]
        for g in range(8):
            moves.append((down_ref.at[j, half, pl.ds(g * 256, 256)], held.at[r, pl.ds(2048 + g * 128, 128), :]))
        copies += [pltpu.make_async_copy(source, target, sem.at[r, n]) for n, (source, target) in enumerate(moves)]
    return copies


def unload_copies(held, packs, sem):
    return [pltpu.make_async_copy(held.at[r], packs[r], sem.at[r, 10]) for r in range(4)]


def attention_kernel(length_ref, q_ref, user_ref, hist_ref, act_ref, kw_ref, tab_ref, vw_ref, gate_ref, up_ref, down_ref, *refs):
    out_ref, packs, (m_ref, l_ref, acc_ref, kwt_ref, tabt_ref, owner_ref, held, sem) = refs[0], refs[1:5], refs[5:]
    step = pl.program_id(0)
    events = CHUNK * pl.num_programs(0)
    offset = lax.axis_index("hist") * events + step * CHUNK

    @pl.when(step == 0)
    def _():
        for copy in pack_copies(gate_ref, up_ref, down_ref, held, sem):
            copy.start()
        m_ref[...] = jnp.full_like(m_ref, -1e29)
        l_ref[...] = jnp.zeros_like(l_ref)
        acc_ref[...] = jnp.zeros_like(acc_ref)
        kwt_ref[...] = jnp.transpose(kw_ref[...].astype(F32)).astype(BF16)
        tabt_ref[...] = jnp.transpose(tab_ref[...].astype(F32)).astype(BF16)
        user = jnp.transpose(jnp.broadcast_to(user_ref[...], (128, 128))) - lax.axis_index("cand") * 2
        owner_ref[0:128, :] = user[:, 0:1]
        owner_ref[128:256, :] = user[:, 0:1]

    @pl.when(step == 3)
    def _():
        for copy in pack_copies(gate_ref, up_ref, down_ref, held, sem):
            copy.wait()
        for copy in unload_copies(held, packs, sem):
            copy.start()

    first = owner_ref[...] == 0
    q = q_ref[...]
    where = lax.broadcasted_iota(jnp.int32, (1, CHUNK), 1) + offset
    scores, values = [], []
    for u in range(2):
        h = hist_ref[u]
        kinds = lax.broadcasted_iota(jnp.int32, (ACTIONS, CHUNK), 0)
        onehot = jnp.where(kinds == act_ref[u : u + 1, :], 1.0, 0.0).astype(BF16)
        keys = dot(kwt_ref[...], h, ((1,), (1,))) + dot(tabt_ref[...], onehot)
        s = dot(q, keys.astype(BF16))
        scores.append(jnp.where(where < length_ref[u], s, -1e30))
        wide = h.astype(F32)
        normed = wide * lax.rsqrt(jnp.mean(wide * wide, axis=1, keepdims=True) + EPS)
        values.append(dot(normed.astype(BF16), vw_ref[...]).astype(BF16))
    s = jnp.where(first, scores[0], scores[1])
    m_old = m_ref[...]
    m_new = jnp.maximum(m_old, jnp.max(s, axis=1, keepdims=True))
    p = jnp.exp2((s - m_new) * SCALE)
    fade = jnp.exp2((m_old - m_new) * SCALE)
    m_ref[...] = m_new
    l_ref[...] = l_ref[...] * fade + jnp.sum(p, axis=1, keepdims=True)
    acc_ref[...] = acc_ref[...] * fade + dot(p.astype(BF16), jnp.concatenate(values, axis=1))

    @pl.when(step == pl.num_programs(0) - 1)
    def _():
        weighted = jnp.where(first, acc_ref[:, 0:128], acc_ref[:, 128:256])
        out_ref[0:256, :] = (weighted / jnp.maximum(l_ref[...], 1e-30)).astype(BF16)
        for n, ref in ((256, m_ref), (272, l_ref)):
            row = jnp.transpose(jnp.broadcast_to(ref[...], (256, 128)))[0:1, :]
            rows = []
            for _ in range(3):
                piece = row.astype(BF16).astype(F32)
                row = row - piece
                rows += [piece[:, 0:128], piece[:, 128:256]]
            rows += [jnp.zeros((10, 128), F32)]
            out_ref[n : n + 16, :] = jnp.concatenate(rows, axis=0).astype(BF16)
        for copy in unload_copies(held, packs, sem):
            copy.wait()


def attention(lengths, queries, user, history, actions, kw, tab, vw, gate, up, down):
    steps = history.shape[1] // CHUNK
    whole = lambda *shape: pl.BlockSpec(shape, lambda i, lim: (0,) * len(shape))
    anywhere = pl.BlockSpec(memory_space=pl.ANY)
    return pl.pallas_call(
        attention_kernel,
        out_shape=[jax.ShapeDtypeStruct((288, 128), BF16)] + [jax.ShapeDtypeStruct((3072, 256), BF16)] * 4,
        grid_spec=pltpu.PrefetchScalarGridSpec(
            num_scalar_prefetch=1,
            grid=(steps,),
            in_specs=[
                whole(256, 128),
                whole(1, 128),
                pl.BlockSpec((2, CHUNK, 128), lambda i, lim: (0, i, 0)),
                pl.BlockSpec((2, CHUNK), lambda i, lim: (0, i)),
                whole(128, 128),
                whole(ACTIONS, 128),
                whole(128, 128),
                anywhere,
                anywhere,
                anywhere,
            ],
            out_specs=[whole(288, 128)] + [anywhere] * 4,
            scratch_shapes=[
                pltpu.VMEM((256, 1), F32),
                pltpu.VMEM((256, 1), F32),
                pltpu.VMEM((256, 256), F32),
                pltpu.VMEM((128, 128), BF16),
                pltpu.VMEM((128, ACTIONS), BF16),
                pltpu.VMEM((256, 1), jnp.int32),
                pltpu.VMEM((4, 3072, 256), BF16),
                pltpu.SemaphoreType.DMA((4, 11)),
            ],
        ),
        compiler_params=pltpu.CompilerParams(dimension_semantics=("arbitrary",), vmem_limit_bytes=58 << 20),
        cost_estimate=pl.CostEstimate(flops=1_000_000, bytes_accessed=100_000, transcendentals=1_000),
        name="attention",
    )(lengths, queries, user, history, actions, kw, tab, vw, gate, up, down)


def merge_kernel(p0, p1, p2, p3, feat_ref, ow_ref, out_ref):
    parts = (p0, p1, p2, p3)

    def column(ref, n):
        pieces = ref[n : n + 16, :].astype(F32)
        rows = pieces[0:2] + (pieces[2:4] + pieces[4:6])
        rows = [jnp.transpose(jnp.broadcast_to(rows[i : i + 1], (128, 128))) for i in range(2)]
        return jnp.concatenate(rows, axis=0)

    maxima = [column(ref, 256) for ref in parts]
    top = jnp.maximum(jnp.maximum(maxima[0], maxima[1]), jnp.maximum(maxima[2], maxima[3]))
    total, weighted = 0.0, 0.0
    for ref, m in zip(parts, maxima):
        share = column(ref, 272) * jnp.exp2((m - top) * SCALE)
        total += share
        weighted += ref[0:256, :].astype(F32) * share
    attended = (weighted / total).astype(BF16)
    y = lax.axis_index("hist")
    for x in range(4):
        columns = pl.ds(pl.multiple_of((4 * x + y) * 128, 128), 128)
        for j in range(2):
            update = dot(attended[j * 128 : (j + 1) * 128], ow_ref[j, :, columns])
            tokens = (feat_ref[j, :, columns].astype(F32) + update).astype(BF16)
            for k in range(2):
                for m in range(4):
                    out_ref[2 * x + k, m * 16 : (m + 1) * 16, j * 128 : (j + 1) * 128] = tokens[
                        m * 32 + k * 16 : m * 32 + k * 16 + 16
                    ]


def merge(parts, feats, ow):
    return pl.pallas_call(
        merge_kernel,
        out_shape=jax.ShapeDtypeStruct((8, 64, 256), BF16),
        compiler_params=pltpu.CompilerParams(vmem_limit_bytes=16 << 20),
        cost_estimate=pl.CostEstimate(flops=70_000_000, bytes_accessed=1_500_000, transcendentals=150_000),
        name="merge",
    )(*parts, feats, ow)


def hidden_part(normed, weights, hidden, p):
    both = dot(normed[...], weights)
    gate, up = both[:, :128], both[:, 128:]
    hidden[:, p * 128 : (p + 1) * 128] = (gate / (1.0 + jnp.exp(-gate)) * up).astype(BF16)


def down_weights(refs, g):
    return jnp.concatenate([ref[g * 128 : (g + 1) * 128, :] for ref in refs], axis=0)


def first_kernel(x_ref, *refs):
    packs, (normed, so_far, hidden, held, sem) = refs[:4], refs[4:]
    copies = [pltpu.make_async_copy(packs[p], held.at[p], sem.at[p]) for p in range(4)]
    for copy in copies:
        copy.start()
    z = lax.axis_index("cand")
    for zb in range(8):
        wide = jnp.concatenate([x_ref[zb, s] for s in range(8)], axis=1).astype(F32)
        rows = (wide * lax.rsqrt(jnp.mean(wide * wide, axis=1, keepdims=True) + EPS)).astype(BF16)
        for m in range(4):
            away = lax.rem((zb % 2) * 4 + m + 8 - z, 8)
            to = pl.multiple_of(away * 64 + (zb // 2) * 16, 16)
            normed[pl.ds(to, 16), :] = rows[m * 16 : (m + 1) * 16]
    for p in range(4):
        copies[p].wait()
        hidden_part(normed, held[p, 0:2048, :], hidden, p)
    downs = [held.at[p, pl.ds(2048, 1024)] for p in range(4)]
    for g in range(8):
        so_far[:, g * 256 : (g + 1) * 256] = dot(hidden[...], down_weights(downs, g))


def middle_kernel(normed, *refs):
    late, (hidden, gu, gu_sem) = refs[:2], refs[2:]
    copies = [pltpu.make_async_copy(late[p].at[pl.ds(0, 2048)], gu.at[p], gu_sem.at[p]) for p in range(2)]
    for copy in copies:
        copy.start()
    for p in range(2):
        copies[p].wait()
        hidden_part(normed, gu[p], hidden, p)


def far_kernel(normed_all, so_far_all, hidden_all, *refs):
    late, swapped, (far_a, far_b, hidden, normed, so_far, downs, sem) = refs[:2], refs[2:4], refs[4:]
    copies = [
        pltpu.make_async_copy(normed_all.at[pl.ds(256, 64)], normed, sem.at[0]),
        pltpu.make_async_copy(so_far_all.at[pl.ds(256, 64)], so_far, sem.at[1]),
    ] + [pltpu.make_async_copy(late[p].at[pl.ds(2048, 1024)], downs.at[p], sem.at[2 + p]) for p in range(2)]
    for copy in copies:
        copy.start()
    hidden[:, 0:256] = hidden_all[256:320, :]
    copies[0].wait()
    for p in range(2):
        hidden_part(normed, swapped[p][0:2048, :], hidden, 2 + p)
    for copy in copies[1:]:
        copy.wait()
    parts = [downs.at[p] for p in range(2)] + [swapped[p].at[pl.ds(2048, 1024)] for p in range(2)]
    for g in range(8):
        columns = so_far[:, g * 256 : (g + 1) * 256] + dot(hidden[...], down_weights(parts, g))
        (far_a, far_b)[g // 4][:, (g % 4) * 256 : (g % 4 + 1) * 256] = columns.astype(BF16)


def near_kernel(normed, so_far, hidden_in, *refs):
    late, swapped, (near, hidden, downs, sem) = refs[:2], refs[2:4], refs[4:]
    copies = [pltpu.make_async_copy(late[p].at[pl.ds(2048, 1024)], downs.at[p], sem.at[p]) for p in range(2)]
    for copy in copies:
        copy.start()
    hidden[:, 0:256] = hidden_in[...]
    for p in range(2):
        hidden_part(normed, swapped[p][0:2048, :], hidden, 2 + p)
    for copy in copies:
        copy.wait()
    parts = [downs.at[p] for p in range(2)] + [swapped[p].at[pl.ds(2048, 1024)] for p in range(2)]
    for g in range(8):
        span = slice(g * 256, (g + 1) * 256)
        columns = (so_far[:, span] + dot(hidden[...], down_weights(parts, g))).astype(BF16)
        for away in range(8):
            near[away, :, span] = columns[away * 64 : (away + 1) * 64]


def gate_kernel(*refs):
    pass


def gated(packs):
    shape = jax.ShapeDtypeStruct((3072, 256), BF16)
    n = len(packs)
    return pl.pallas_call(
        gate_kernel,
        out_shape=[shape] * n,
        in_specs=[pl.BlockSpec(memory_space=pl.ANY)] * n,
        out_specs=[pl.BlockSpec(memory_space=pl.ANY)] * n,
        input_output_aliases={i: i for i in range(n)},
        cost_estimate=pl.CostEstimate(flops=200_000_000_000, bytes_accessed=1000, transcendentals=0),
        name="gate",
    )(*packs)


VMEM_SPEC = pl.BlockSpec(memory_space=pltpu.VMEM)
ANY_SPEC = pl.BlockSpec(memory_space=pl.ANY)
FFN_PARAMS = pltpu.CompilerParams(vmem_limit_bytes=54 << 20)
FFN_COST = pl.CostEstimate(flops=3_000_000_000, bytes_accessed=8_000_000, transcendentals=300_000)


def feed_forward_first(x, packs):
    return pl.pallas_call(
        first_kernel,
        out_shape=[jax.ShapeDtypeStruct((512, 2048), BF16), jax.ShapeDtypeStruct((512, 2048), F32)],
        in_specs=[VMEM_SPEC] + [ANY_SPEC] * 4,
        out_specs=[VMEM_SPEC] * 2,
        scratch_shapes=[
            pltpu.VMEM((512, 512), BF16),
            pltpu.VMEM((4, 3072, 256), BF16),
            pltpu.SemaphoreType.DMA((4,)),
        ],
        compiler_params=FFN_PARAMS,
        cost_estimate=FFN_COST,
        name="feed_forward_first",
    )(x, *packs)


def feed_forward_middle(normed, late):
    return pl.pallas_call(
        middle_kernel,
        out_shape=jax.ShapeDtypeStruct((512, 256), BF16),
        in_specs=[VMEM_SPEC] + [ANY_SPEC] * 2,
        out_specs=VMEM_SPEC,
        scratch_shapes=[pltpu.VMEM((2, 2048, 256), BF16), pltpu.SemaphoreType.DMA((2,))],
        compiler_params=FFN_PARAMS,
        cost_estimate=FFN_COST,
        name="feed_forward_middle",
    )(normed, *late)


def feed_forward_far(normed, so_far, hidden, late, swapped):
    return pl.pallas_call(
        far_kernel,
        out_shape=[jax.ShapeDtypeStruct((64, 1024), BF16)] * 2,
        in_specs=[ANY_SPEC, ANY_SPEC, VMEM_SPEC, ANY_SPEC, ANY_SPEC, VMEM_SPEC, VMEM_SPEC],
        out_specs=[VMEM_SPEC] * 2,
        scratch_shapes=[
            pltpu.VMEM((64, 512), BF16),
            pltpu.VMEM((64, 2048), BF16),
            pltpu.VMEM((64, 2048), F32),
            pltpu.VMEM((2, 1024, 256), BF16),
            pltpu.SemaphoreType.DMA((4,)),
        ],
        compiler_params=pltpu.CompilerParams(vmem_limit_bytes=28 << 20),
        cost_estimate=FFN_COST,
        name="feed_forward_far",
    )(normed, so_far, hidden, *late, *swapped)


def feed_forward_near(normed, so_far, hidden, late, swapped):
    return pl.pallas_call(
        near_kernel,
        out_shape=jax.ShapeDtypeStruct((8, 64, 2048), BF16),
        in_specs=[VMEM_SPEC] * 3 + [ANY_SPEC, ANY_SPEC, VMEM_SPEC, VMEM_SPEC],
        out_specs=VMEM_SPEC,
        scratch_shapes=[
            pltpu.VMEM((512, 512), BF16),
            pltpu.VMEM((2, 1024, 256), BF16),
            pltpu.SemaphoreType.DMA((2,)),
        ],
        compiler_params=pltpu.CompilerParams(vmem_limit_bytes=28 << 20),
        cost_estimate=FFN_COST,
        name="feed_forward_near",
    )(normed, so_far, hidden, *late, *swapped)


def exchange_pairs(r, reverse):
    pairs = []
    for y in range(HIST):
        for t in range(TOK):
            x, c = t // 2, t % 2
            q = y ^ r
            source, target = (y, 2 * x + c), (2 * c + q // 2, 2 * x + q % 2)
            if reverse:
                source, target = target, source
            pairs.append((source[0] * TOK + source[1], target[0] * TOK + target[1]))
    return pairs


def shards(
    features,
    query_weight,
    output_weight,
    history,
    actions,
    lengths,
    cand_user,
    key_weight,
    action_table,
    value_weight,
    gate_weight,
    up_weight,
    down_weight,
    tower_weight,
    tower_bias,
    head_weight,
):
    y, tok, z = lax.axis_index("hist"), lax.axis_index("tok"), lax.axis_index("cand")
    core = tok % 2
    both = ("hist", "tok")

    feats = jnp.swapaxes(features, 0, 1)
    queries = jnp.einsum("tbd,tdk->tbk", feats, query_weight, preferred_element_type=F32).astype(BF16)
    part, *packs = attention(
        lengths,
        queries.reshape(256, 128),
        cand_user[None, :],
        history,
        actions,
        key_weight,
        action_table,
        value_weight,
        gate_weight,
        up_weight,
        down_weight,
    )
    parts = [part] + [lax.ppermute(part, "hist", [(i, (i + d) % HIST) for i in range(HIST)]) for d in (1, 2, 3)]
    packs, parts = lax.optimization_barrier((packs, parts))
    packs = [lax.ppermute(pack, both, exchange_pairs(r, False)) for r, pack in enumerate(packs)]

    outgoing = merge(parts, feats, output_weight)
    mixed = lax.all_to_all(outgoing, "tok", split_axis=0, concat_axis=0, tiled=True)
    gathered = lax.all_gather(mixed[None], "cand", axis=0, tiled=True)

    swap = lambda v: lax.ppermute(v, "tok", [(i, i ^ 1) for i in range(TOK)])
    early = list(gated([packs[0], packs[2]]))
    early += [swap(v) for v in early]
    normed, so_far = feed_forward_first(gathered, early)
    late, normed = lax.optimization_barrier(([packs[1], packs[3]], normed))
    late = list(gated(late))
    swapped = [swap(v) for v in late]
    hidden = feed_forward_middle(normed, late)
    far_a, far_b = feed_forward_far(normed, so_far, hidden, late, swapped)
    near = feed_forward_near(normed, so_far, hidden, late, swapped)
    right = [(i, (i + 1) % CAND) for i in range(CAND)]
    left = [(i, (i - 1) % CAND) for i in range(CAND)]
    wide = lambda v: v.astype(F32)
    add = lambda v, w: (wide(v) + wide(w)).astype(BF16)
    up, down = lax.ppermute(far_a, "cand", right), lax.ppermute(far_b, "cand", left)
    up, down = jnp.pad(up, ((0, 0), (0, 1024))), jnp.pad(down, ((0, 0), (1024, 0)))
    for i in (3, 2, 1):
        up, down = lax.optimization_barrier((add(near[i], up), add(near[8 - i], down)))
        up, down = lax.ppermute(up, "cand", right), lax.ppermute(down, "cand", left)
    residual = lax.dynamic_slice(
        gathered.reshape(4, 2, 8, 4, 16, 256), (0, z // 4, 0, z % 4, 0, 0), (4, 1, 8, 1, 16, 256)
    ).reshape(4, 8, 16, 256)
    residual = jnp.swapaxes(residual, 1, 2).reshape(64, 2048)
    block = (wide(residual) + (wide(near[0]) + wide(up) + wide(down))).astype(BF16).reshape(4, 16, 2048)

    arrived = []
    mine = (y % 2) * 2 + core
    for r in range(4):
        send = lax.dynamic_index_in_dim(block, mine ^ r, 0, keepdims=False)
        arrived.append(lax.ppermute(send, both, exchange_pairs(r, True)))
    arrived = jnp.stack(arrived)
    quarters = [lax.dynamic_index_in_dim(arrived, y ^ q, 0, keepdims=False) for q in range(4)]
    tokens = [jnp.concatenate(quarters[2 * j : 2 * j + 2], axis=0) for j in range(2)]
    layer_out = jnp.stack(tokens, axis=1)

    tower_part = dot(tokens[0], tower_weight[0]) + dot(tokens[1], tower_weight[1])
    tower_part += swap(tower_part)
    tower_sum = tower_part
    for d in (2, 4, 6):
        tower_sum += lax.ppermute(tower_part, "tok", [(i, i ^ d) for i in range(TOK)])
    tower_hidden = jax.nn.silu(tower_sum + tower_bias).astype(BF16)
    task_scores = jnp.dot(tower_hidden, head_weight, preferred_element_type=F32)
    return (layer_out, task_scores)


def solution(mesh):
    in_specs = (
        P("cand", "tok", None),
        P("tok", None, None),
        P("tok", None, None),
        P("cand", "hist", None),
        P("cand", "hist"),
        P("cand"),
        P("cand"),
        P(),
        P(),
        P(),
        P("tok", None, ("hist", "cand")),
        P("tok", None, ("hist", "cand")),
        P("tok", ("hist", "cand"), None),
        P("tok", None, None),
        P(),
        P(),
    )
    out_specs = (P(("hist", "cand"), "tok", None), P(("hist", "cand"), None))
    return jax.shard_map(shards, mesh=mesh, in_specs=in_specs, out_specs=out_specs, check_vma=False)
```

```python
import jax
import jax.numpy as jnp
from jax import lax
from jax.experimental import pallas as pl
from jax.experimental.pallas import tpu as pltpu
from jax.sharding import PartitionSpec as P

EPS = 1e-06
DK = 128
ACTIONS = 16
HIST, TOK, CAND = 4, 8, 8
SCALE = 1.5 * DK ** (-0.5) * 1.4426950408889634
CHUNK = 512
F32 = jnp.float32
BF16 = jnp.bfloat16


def dot(a, b, dims=((1,), (0,))):
    return lax.dot_general(a, b, (dims, ((), ())), preferred_element_type=F32)


def pack_copies(gate_ref, up_ref, down_ref, held, sem):
    y = lax.axis_index("hist")
    copies = []
    for r in range(4):
        j, k = lax.rem(y // 2 + r // 2, 2), lax.rem(y + r, 2)
        half = pl.ds(pl.multiple_of(k * 128, 128), 128)
        moves = [
            (gate_ref.at[j, :, half], held.at[r, pl.ds(0, 2048), pl.ds(0, 128)]),
            (up_ref.at[j, :, half], held.at[r, pl.ds(0, 2048), pl.ds(128, 128)]),
        ]
        for g in range(8):
            moves.append((down_ref.at[j, half, pl.ds(g * 256, 256)], held.at[r, pl.ds(2048 + g * 128, 128), :]))
        copies += [pltpu.make_async_copy(source, target, sem.at[r, n]) for n, (source, target) in enumerate(moves)]
    return copies


def unload_copies(held, packs, sem):
    return [pltpu.make_async_copy(held.at[r], packs[r], sem.at[r, 10]) for r in range(4)]


def attention_kernel(length_ref, q_ref, user_ref, hist_ref, act_ref, kw_ref, tab_ref, vw_ref, gate_ref, up_ref, down_ref, *refs):
    out_ref, packs, (m_ref, l_ref, acc_ref, kwt_ref, tabt_ref, owner_ref, held, sem) = refs[0], refs[1:5], refs[5:]
    step = pl.program_id(0)
    events = CHUNK * pl.num_programs(0)
    offset = lax.axis_index("hist") * events + step * CHUNK

    @pl.when(step == 0)
    def _():
        for copy in pack_copies(gate_ref, up_ref, down_ref, held, sem):
            copy.start()
        m_ref[...] = jnp.full_like(m_ref, -1e29)
        l_ref[...] = jnp.zeros_like(l_ref)
        acc_ref[...] = jnp.zeros_like(acc_ref)
        kwt_ref[...] = jnp.transpose(kw_ref[...].astype(F32)).astype(BF16)
        tabt_ref[...] = jnp.transpose(tab_ref[...].astype(F32)).astype(BF16)
        user = jnp.transpose(jnp.broadcast_to(user_ref[...], (128, 128))) - lax.axis_index("cand") * 2
        owner_ref[0:128, :] = user[:, 0:1]
        owner_ref[128:256, :] = user[:, 0:1]

    @pl.when(step == 1)
    def _():
        for copy in pack_copies(gate_ref, up_ref, down_ref, held, sem):
            copy.wait()
        for copy in unload_copies(held, packs, sem):
            copy.start()

    first = owner_ref[...] == 0
    q = q_ref[...]
    where = lax.broadcasted_iota(jnp.int32, (1, CHUNK), 1) + offset
    scores, values = [], []
    for u in range(2):
        h = hist_ref[u]
        kinds = lax.broadcasted_iota(jnp.int32, (ACTIONS, CHUNK), 0)
        onehot = jnp.where(kinds == act_ref[u : u + 1, :], 1.0, 0.0).astype(BF16)
        keys = dot(kwt_ref[...], h, ((1,), (1,))) + dot(tabt_ref[...], onehot)
        s = dot(q, keys.astype(BF16))
        scores.append(jnp.where(where < length_ref[u], s, -1e30))
        wide = h.astype(F32)
        normed = wide * lax.rsqrt(jnp.mean(wide * wide, axis=1, keepdims=True) + EPS)
        values.append(dot(normed.astype(BF16), vw_ref[...]).astype(BF16))
    s = jnp.where(first, scores[0], scores[1])
    m_old = m_ref[...]
    m_new = jnp.maximum(m_old, jnp.max(s, axis=1, keepdims=True))
    p = jnp.exp2((s - m_new) * SCALE)
    fade = jnp.exp2((m_old - m_new) * SCALE)
    m_ref[...] = m_new
    l_ref[...] = l_ref[...] * fade + jnp.sum(p, axis=1, keepdims=True)
    acc_ref[...] = acc_ref[...] * fade + dot(p.astype(BF16), jnp.concatenate(values, axis=1))

    @pl.when(step == pl.num_programs(0) - 1)
    def _():
        weighted = jnp.where(first, acc_ref[:, 0:128], acc_ref[:, 128:256])
        out_ref[0:256, :] = (weighted / jnp.maximum(l_ref[...], 1e-30)).astype(BF16)
        for n, ref in ((256, m_ref), (272, l_ref)):
            row = jnp.transpose(jnp.broadcast_to(ref[...], (256, 128)))[0:1, :]
            rows = []
            for _ in range(3):
                piece = row.astype(BF16).astype(F32)
                row = row - piece
                rows += [piece[:, 0:128], piece[:, 128:256]]
            rows += [jnp.zeros((10, 128), F32)]
            out_ref[n : n + 16, :] = jnp.concatenate(rows, axis=0).astype(BF16)
        for copy in unload_copies(held, packs, sem):
            copy.wait()


def attention(lengths, queries, user, history, actions, kw, tab, vw, gate, up, down):
    steps = history.shape[1] // CHUNK
    whole = lambda *shape: pl.BlockSpec(shape, lambda i, lim: (0,) * len(shape))
    anywhere = pl.BlockSpec(memory_space=pl.ANY)
    return pl.pallas_call(
        attention_kernel,
        out_shape=[jax.ShapeDtypeStruct((288, 128), BF16)] + [jax.ShapeDtypeStruct((3072, 256), BF16)] * 4,
        grid_spec=pltpu.PrefetchScalarGridSpec(
            num_scalar_prefetch=1,
            grid=(steps,),
            in_specs=[
                whole(256, 128),
                whole(1, 128),
                pl.BlockSpec((2, CHUNK, 128), lambda i, lim: (0, i, 0)),
                pl.BlockSpec((2, CHUNK), lambda i, lim: (0, i)),
                whole(128, 128),
                whole(ACTIONS, 128),
                whole(128, 128),
                anywhere,
                anywhere,
                anywhere,
            ],
            out_specs=[whole(288, 128)] + [anywhere] * 4,
            scratch_shapes=[
                pltpu.VMEM((256, 1), F32),
                pltpu.VMEM((256, 1), F32),
                pltpu.VMEM((256, 256), F32),
                pltpu.VMEM((128, 128), BF16),
                pltpu.VMEM((128, ACTIONS), BF16),
                pltpu.VMEM((256, 1), jnp.int32),
                pltpu.VMEM((4, 3072, 256), BF16),
                pltpu.SemaphoreType.DMA((4, 11)),
            ],
        ),
        compiler_params=pltpu.CompilerParams(dimension_semantics=("arbitrary",), vmem_limit_bytes=58 << 20),
        cost_estimate=pl.CostEstimate(flops=1_000_000, bytes_accessed=100_000, transcendentals=1_000),
        name="attention",
    )(lengths, queries, user, history, actions, kw, tab, vw, gate, up, down)


def merge_kernel(p0, p1, p2, p3, feat_ref, ow_ref, out_ref):
    parts = (p0, p1, p2, p3)

    def column(ref, n):
        pieces = ref[n : n + 16, :].astype(F32)
        rows = pieces[0:2] + (pieces[2:4] + pieces[4:6])
        rows = [jnp.transpose(jnp.broadcast_to(rows[i : i + 1], (128, 128))) for i in range(2)]
        return jnp.concatenate(rows, axis=0)

    maxima = [column(ref, 256) for ref in parts]
    top = jnp.maximum(jnp.maximum(maxima[0], maxima[1]), jnp.maximum(maxima[2], maxima[3]))
    total, weighted = 0.0, 0.0
    for ref, m in zip(parts, maxima):
        share = column(ref, 272) * jnp.exp2((m - top) * SCALE)
        total += share
        weighted += ref[0:256, :].astype(F32) * share
    attended = (weighted / total).astype(BF16)
    y = lax.axis_index("hist")
    for x in range(4):
        columns = pl.ds(pl.multiple_of((4 * x + y) * 128, 128), 128)
        for j in range(2):
            update = dot(attended[j * 128 : (j + 1) * 128], ow_ref[j, :, columns])
            tokens = (feat_ref[j, :, columns].astype(F32) + update).astype(BF16)
            for k in range(2):
                for m in range(4):
                    out_ref[2 * x + k, m * 16 : (m + 1) * 16, j * 128 : (j + 1) * 128] = tokens[
                        m * 32 + k * 16 : m * 32 + k * 16 + 16
                    ]


def merge(parts, feats, ow):
    return pl.pallas_call(
        merge_kernel,
        out_shape=jax.ShapeDtypeStruct((8, 64, 256), BF16),
        compiler_params=pltpu.CompilerParams(vmem_limit_bytes=16 << 20),
        cost_estimate=pl.CostEstimate(flops=70_000_000, bytes_accessed=1_500_000, transcendentals=150_000),
        name="merge",
    )(*parts, feats, ow)


def hidden_part(normed, weights, hidden, p):
    both = dot(normed[...], weights)
    gate, up = both[:, :128], both[:, 128:]
    hidden[:, p * 128 : (p + 1) * 128] = (gate / (1.0 + jnp.exp(-gate)) * up).astype(BF16)


def down_weights(refs, g):
    return jnp.concatenate([ref[g * 128 : (g + 1) * 128, :] for ref in refs], axis=0)


def first_kernel(x_ref, *refs):
    packs, (normed, so_far, hidden, held, sem) = refs[:4], refs[4:]
    copies = [pltpu.make_async_copy(packs[p], held.at[p], sem.at[p]) for p in range(4)]
    for copy in copies:
        copy.start()
    z = lax.axis_index("cand")
    for zb in range(8):
        wide = jnp.concatenate([x_ref[zb, s] for s in range(8)], axis=1).astype(F32)
        rows = (wide * lax.rsqrt(jnp.mean(wide * wide, axis=1, keepdims=True) + EPS)).astype(BF16)
        for m in range(4):
            away = lax.rem((zb % 2) * 4 + m + 8 - z, 8)
            to = pl.multiple_of(away * 64 + (zb // 2) * 16, 16)
            normed[pl.ds(to, 16), :] = rows[m * 16 : (m + 1) * 16]
    for p in range(4):
        copies[p].wait()
        hidden_part(normed, held[p, 0:2048, :], hidden, p)
    downs = [held.at[p, pl.ds(2048, 1024)] for p in range(4)]
    for g in range(8):
        so_far[:, g * 256 : (g + 1) * 256] = dot(hidden[...], down_weights(downs, g))


def middle_kernel(normed, *refs):
    late, (hidden, gu, gu_sem) = refs[:2], refs[2:]
    copies = [pltpu.make_async_copy(late[p].at[pl.ds(0, 2048)], gu.at[p], gu_sem.at[p]) for p in range(2)]
    for copy in copies:
        copy.start()
    for p in range(2):
        copies[p].wait()
        hidden_part(normed, gu[p], hidden, p)


def far_kernel(normed_all, so_far_all, hidden_all, *refs):
    late, swapped, (far_a, far_b, hidden, normed, so_far, downs, sem) = refs[:2], refs[2:4], refs[4:]
    copies = [
        pltpu.make_async_copy(normed_all.at[pl.ds(256, 64)], normed, sem.at[0]),
        pltpu.make_async_copy(so_far_all.at[pl.ds(256, 64)], so_far, sem.at[1]),
    ] + [pltpu.make_async_copy(late[p].at[pl.ds(2048, 1024)], downs.at[p], sem.at[2 + p]) for p in range(2)]
    copies.append(pltpu.make_async_copy(hidden_all.at[pl.ds(256, 64)], hidden.at[:, pl.ds(0, 256)], sem.at[4]))
    for copy in copies:
        copy.start()
    copies[0].wait()
    for p in range(2):
        hidden_part(normed, swapped[p][0:2048, :], hidden, 2 + p)
    for copy in copies[1:]:
        copy.wait()
    parts = [downs.at[p] for p in range(2)] + [swapped[p].at[pl.ds(2048, 1024)] for p in range(2)]
    for g in range(8):
        columns = so_far[:, g * 256 : (g + 1) * 256] + dot(hidden[...], down_weights(parts, g))
        (far_a, far_b)[g // 4][:, (g % 4) * 256 : (g % 4 + 1) * 256] = columns.astype(BF16)


def near_kernel(normed, so_far, hidden_in, *refs):
    late, swapped, (near, hidden, downs, sem) = refs[:2], refs[2:4], refs[4:]
    copies = [pltpu.make_async_copy(late[p].at[pl.ds(2048, 1024)], downs.at[p], sem.at[p]) for p in range(2)]
    for copy in copies:
        copy.start()
    hidden[:, 0:256] = hidden_in[...]
    for p in range(2):
        hidden_part(normed, swapped[p][0:2048, :], hidden, 2 + p)
    for copy in copies:
        copy.wait()
    parts = [downs.at[p] for p in range(2)] + [swapped[p].at[pl.ds(2048, 1024)] for p in range(2)]
    for g in range(8):
        span = slice(g * 256, (g + 1) * 256)
        columns = (so_far[:, span] + dot(hidden[...], down_weights(parts, g))).astype(BF16)
        for away in range(8):
            near[away, :, span] = columns[away * 64 : (away + 1) * 64]


def gate_kernel(*refs):
    pass


def gated(packs):
    shape = jax.ShapeDtypeStruct((3072, 256), BF16)
    n = len(packs)
    return pl.pallas_call(
        gate_kernel,
        out_shape=[shape] * n,
        in_specs=[pl.BlockSpec(memory_space=pl.ANY)] * n,
        out_specs=[pl.BlockSpec(memory_space=pl.ANY)] * n,
        input_output_aliases={i: i for i in range(n)},
        cost_estimate=pl.CostEstimate(flops=200_000_000_000, bytes_accessed=1000, transcendentals=0),
        name="gate",
    )(*packs)


VMEM_SPEC = pl.BlockSpec(memory_space=pltpu.VMEM)
ANY_SPEC = pl.BlockSpec(memory_space=pl.ANY)
FFN_PARAMS = pltpu.CompilerParams(vmem_limit_bytes=54 << 20)
FFN_COST = pl.CostEstimate(flops=3_000_000_000, bytes_accessed=8_000_000, transcendentals=300_000)


def feed_forward_first(x, packs):
    return pl.pallas_call(
        first_kernel,
        out_shape=[jax.ShapeDtypeStruct((512, 2048), BF16), jax.ShapeDtypeStruct((512, 2048), F32)],
        in_specs=[VMEM_SPEC] + [ANY_SPEC] * 4,
        out_specs=[VMEM_SPEC] * 2,
        scratch_shapes=[
            pltpu.VMEM((512, 512), BF16),
            pltpu.VMEM((4, 3072, 256), BF16),
            pltpu.SemaphoreType.DMA((4,)),
        ],
        compiler_params=FFN_PARAMS,
        cost_estimate=FFN_COST,
        name="feed_forward_first",
    )(x, *packs)


def feed_forward_middle(normed, late):
    return pl.pallas_call(
        middle_kernel,
        out_shape=jax.ShapeDtypeStruct((512, 256), BF16),
        in_specs=[VMEM_SPEC] + [ANY_SPEC] * 2,
        out_specs=VMEM_SPEC,
        scratch_shapes=[pltpu.VMEM((2, 2048, 256), BF16), pltpu.SemaphoreType.DMA((2,))],
        compiler_params=FFN_PARAMS,
        cost_estimate=FFN_COST,
        name="feed_forward_middle",
    )(normed, *late)


def feed_forward_far(normed, so_far, hidden, late, swapped):
    return pl.pallas_call(
        far_kernel,
        out_shape=[jax.ShapeDtypeStruct((64, 1024), BF16)] * 2,
        in_specs=[ANY_SPEC] * 5 + [VMEM_SPEC] * 2,
        out_specs=[VMEM_SPEC] * 2,
        scratch_shapes=[
            pltpu.VMEM((64, 512), BF16),
            pltpu.VMEM((64, 2048), BF16),
            pltpu.VMEM((64, 2048), F32),
            pltpu.VMEM((2, 1024, 256), BF16),
            pltpu.SemaphoreType.DMA((5,)),
        ],
        compiler_params=pltpu.CompilerParams(vmem_limit_bytes=28 << 20),
        cost_estimate=FFN_COST,
        name="feed_forward_far",
    )(normed, so_far, hidden, *late, *swapped)


def feed_forward_near(normed, so_far, hidden, late, swapped):
    return pl.pallas_call(
        near_kernel,
        out_shape=jax.ShapeDtypeStruct((8, 64, 2048), BF16),
        in_specs=[VMEM_SPEC] * 3 + [ANY_SPEC, ANY_SPEC, VMEM_SPEC, VMEM_SPEC],
        out_specs=VMEM_SPEC,
        scratch_shapes=[
            pltpu.VMEM((512, 512), BF16),
            pltpu.VMEM((2, 1024, 256), BF16),
            pltpu.SemaphoreType.DMA((2,)),
        ],
        compiler_params=pltpu.CompilerParams(vmem_limit_bytes=28 << 20),
        cost_estimate=FFN_COST,
        name="feed_forward_near",
    )(normed, so_far, hidden, *late, *swapped)


def exchange_pairs(r, reverse):
    pairs = []
    for y in range(HIST):
        for t in range(TOK):
            x, c = t // 2, t % 2
            q = y ^ r
            source, target = (y, 2 * x + c), (2 * c + q // 2, 2 * x + q % 2)
            if reverse:
                source, target = target, source
            pairs.append((source[0] * TOK + source[1], target[0] * TOK + target[1]))
    return pairs


def shards(
    features,
    query_weight,
    output_weight,
    history,
    actions,
    lengths,
    cand_user,
    key_weight,
    action_table,
    value_weight,
    gate_weight,
    up_weight,
    down_weight,
    tower_weight,
    tower_bias,
    head_weight,
):
    y, tok, z = lax.axis_index("hist"), lax.axis_index("tok"), lax.axis_index("cand")
    core = tok % 2
    both = ("hist", "tok")

    feats = jnp.swapaxes(features, 0, 1)
    queries = jnp.einsum("tbd,tdk->tbk", feats, query_weight, preferred_element_type=F32).astype(BF16)
    part, *packs = attention(
        lengths,
        queries.reshape(256, 128),
        cand_user[None, :],
        history,
        actions,
        key_weight,
        action_table,
        value_weight,
        gate_weight,
        up_weight,
        down_weight,
    )
    parts = [part] + [lax.ppermute(part, "hist", [(i, (i + d) % HIST) for i in range(HIST)]) for d in (1, 2, 3)]
    packs, parts = lax.optimization_barrier((packs, parts))
    packs = [lax.ppermute(pack, both, exchange_pairs(r, False)) for r, pack in enumerate(packs)]

    outgoing = merge(parts, feats, output_weight)
    mixed = lax.all_to_all(outgoing, "tok", split_axis=0, concat_axis=0, tiled=True)
    gathered = lax.all_gather(mixed[None], "cand", axis=0, tiled=True)

    swap = lambda v: lax.ppermute(v, "tok", [(i, i ^ 1) for i in range(TOK)])
    early = list(gated([packs[0], packs[2]]))
    early += [swap(v) for v in early]
    normed, so_far = feed_forward_first(gathered, early)
    late, normed = lax.optimization_barrier(([packs[1], packs[3]], normed))
    late = list(gated(late))
    swapped = [swap(v) for v in late]
    hidden = feed_forward_middle(normed, late)
    far_a, far_b = feed_forward_far(normed, so_far, hidden, late, swapped)
    near = feed_forward_near(normed, so_far, hidden, late, swapped)
    right = [(i, (i + 1) % CAND) for i in range(CAND)]
    left = [(i, (i - 1) % CAND) for i in range(CAND)]
    wide = lambda v: v.astype(F32)
    add = lambda v, w: (wide(v) + wide(w)).astype(BF16)
    up, down = lax.ppermute(far_a, "cand", right), lax.ppermute(far_b, "cand", left)
    up, down = jnp.pad(up, ((0, 0), (0, 1024))), jnp.pad(down, ((0, 0), (1024, 0)))
    for i in (3, 2, 1):
        up, down = lax.optimization_barrier((add(near[i], up), add(near[8 - i], down)))
        up, down = lax.ppermute(up, "cand", right), lax.ppermute(down, "cand", left)
    residual = lax.dynamic_slice(
        gathered.reshape(4, 2, 8, 4, 16, 256), (0, z // 4, 0, z % 4, 0, 0), (4, 1, 8, 1, 16, 256)
    ).reshape(4, 8, 16, 256)
    residual = jnp.swapaxes(residual, 1, 2).reshape(64, 2048)
    block = (wide(residual) + (wide(near[0]) + wide(up) + wide(down))).astype(BF16).reshape(4, 16, 2048)

    arrived = []
    mine = (y % 2) * 2 + core
    for r in range(4):
        send = lax.dynamic_index_in_dim(block, mine ^ r, 0, keepdims=False)
        arrived.append(lax.ppermute(send, both, exchange_pairs(r, True)))
    arrived = jnp.stack(arrived)
    quarters = [lax.dynamic_index_in_dim(arrived, y ^ q, 0, keepdims=False) for q in range(4)]
    tokens = [jnp.concatenate(quarters[2 * j : 2 * j + 2], axis=0) for j in range(2)]
    layer_out = jnp.stack(tokens, axis=1)

    tower_part = dot(tokens[0], tower_weight[0]) + dot(tokens[1], tower_weight[1])
    tower_part += swap(tower_part)
    tower_sum = tower_part
    for d in (2, 4, 6):
        tower_sum += lax.ppermute(tower_part, "tok", [(i, i ^ d) for i in range(TOK)])
    tower_hidden = jax.nn.silu(tower_sum + tower_bias).astype(BF16)
    task_scores = jnp.dot(tower_hidden, head_weight, preferred_element_type=F32)
    return (layer_out, task_scores)


def solution(mesh):
    in_specs = (
        P("cand", "tok", None),
        P("tok", None, None),
        P("tok", None, None),
        P("cand", "hist", None),
        P("cand", "hist"),
        P("cand"),
        P("cand"),
        P(),
        P(),
        P(),
        P("tok", None, ("hist", "cand")),
        P("tok", None, ("hist", "cand")),
        P("tok", ("hist", "cand"), None),
        P("tok", None, None),
        P(),
        P(),
    )
    out_specs = (P(("hist", "cand"), "tok", None), P(("hist", "cand"), None))
    return jax.shard_map(shards, mesh=mesh, in_specs=in_specs, out_specs=out_specs, check_vma=False)
```
